32 devices in a mesh: dp: 4 (over y, core), graph: 8 (over z, x).
Axes of the slice: x: 2, y: 2, z: 4, core: 2. Of those that a mesh axis runs over, the one named last changes fastest.
Arguments:
- node_features: bfloat16 [128, 49, 128], P(('dp', 'graph')), may hold values from -6 to 6
- cotangent: bfloat16 [128, 49, 128], P(('dp', 'graph')), may hold values from -0.59765625 to 0.59765625
- wigner: float32 [235, 4096], P(None, ('dp', 'graph')), may hold values from -2.4 to 2.4
- w_zero: bfloat16 [896, 896], replicated, may hold values from -0.1875 to 0.1875
- w_one_re: bfloat16 [768, 768], replicated, may hold values from -0.15625 to 0.15625
- w_one_im: bfloat16 [768, 768], replicated, may hold values from -0.15625 to 0.15625
- w_two_re: bfloat16 [640, 640], replicated, may hold values from -0.15625 to 0.15625
- w_two_im: bfloat16 [640, 640], replicated, may hold values from -0.15625 to 0.15625
- w_attn: bfloat16 [896, 8], replicated, may hold values from -0.1875 to 0.1875
- src_slot: int32 [4096], P(('dp', 'graph')), may hold values from 0 to 15
- dst_node: int32 [4096], P(('dp', 'graph')), may hold values from 0 to 3
- request: int32 [32, 8, 2], P(('dp', 'graph')), may hold values from 0 to 3, as said below
- edge_count: int32 [32], P(('dp', 'graph')), may hold values from 1 to 128, 2560 in all
Outputs:
- node_grad: float32 [128, 49, 128], P(('dp', 'graph'))
- grad_zero: float32 [896, 896], P('graph')
- grad_one_re: float32 [768, 768], P('graph')
- grad_one_im: float32 [768, 768], P('graph')
- grad_two_re: float32 [640, 640], P('graph')
- grad_two_im: float32 [640, 640], P('graph')
- grad_attn: float32 [896, 8], P('graph')
The draws below stay inside these ranges and needn't reach their ends.
Inputs may be any that keep to these rules, and one draw needn't show every extreme that they name: request[k, p] holds 2 distinct nodes, numbered within device p of device k's data group, that device k reads from device p. The first edge_count[k] edges of device k are live and the rest are padding; some device has 128.
All inputs are finite; a program needn't handle non-finite values.
Results may differ from the reference program's by a relative error of at most 0.014.
Values may be sent and summed in bfloat16 or wider, within the bound.
A program may use at most 128 MiB of HBM per device.

```python
import math
import jax
import jax.numpy as jnp
import numpy as np
from jax import lax

LMAX = 6
MMAX = 2
C = 128
H = 8
EDGE_DEV = 128
NODE_DEV = 4
SLOTS = 2
NCOEF = 49
WIG = 235
SHARDS = 32
GROUP = 8
NODES = 128
EDGES = 4096
FETCHED = 16
N_DP = 4
N_GRAPH = 8


def draw_request(key, part):
    scores = jax.random.randint(key, (SHARDS, GROUP, NODE_DEV), 0, 1 << 20, dtype=jnp.int32) * NODE_DEV + jnp.arange(NODE_DEV, dtype=jnp.int32)
    _, picked = lax.top_k(scores, SLOTS)
    return picked.astype(jnp.int32)


def place_ends(array, stream_key, least, largest):
    longest = array.shape.index(max(array.shape))
    spots = []
    for shift in (0, 1):
        where = [jax.random.randint(jax.random.fold_in(stream_key, axis), (), 0, length) for axis, length in enumerate(array.shape)]
        where[longest] = (where[longest] + shift) % array.shape[longest]
        spots.append(tuple(where))
    return array.at[spots[0]].set(least).at[spots[1]].set(largest)


def steps_of(stream_key, dims, cuts, smallest, top_value):
    loudness = 1.0
    for dim, blocks in cuts:
        draws = jax.random.uniform(jax.random.fold_in(jax.random.fold_in(stream_key, 6), dim), (blocks,), jnp.float32, smallest / len(cuts), top_value / len(cuts))
        loudness = loudness * jnp.repeat(jnp.exp(draws), dims[dim] // blocks).reshape((-1,) + (1,) * (len(dims) - 1 - dim))
    return loudness


def split_up(count, total, reach, slope):
    loads = [(1 << 20) // math.isqrt(rank ** slope) + 1 for rank in range(2, count + 1)]
    spare, given = total - reach - (count - 1), [1] * (count - 1)
    while spare > 0:
        free = [i for i in range(count - 1) if given[i] < reach]
        mass, budget = sum([loads[i] for i in free]), spare
        for i in free:
            addition = min(reach - given[i], max(1, budget * loads[i] // mass), spare)
            given[i] = given[i] + addition
            spare = spare - addition
    return np.array([reach] + given)


def uneven(rng, count, total, most, lean):
    if count == 2:
        one = jax.random.randint(rng, (), max(1, total - most), min(most, total - 1) + 1)
        return jnp.stack([one, total - one])
    lengths = jnp.asarray(split_up(count, total, most, lean), jnp.int32)
    twos = (count - 1) // 2
    source_of, taker = lengths[1:1 + 2 * twos:2], lengths[2:2 + 2 * twos:2]
    margin = jnp.minimum(source_of - 1, most - taker)
    passed = jax.random.randint(jax.random.fold_in(rng, 1), (twos,), 0, 1 << 20) % (margin + 1)
    lengths = lengths.at[1:1 + 2 * twos:2].set(source_of - passed).at[2:2 + 2 * twos:2].set(taker + passed)
    return lengths[jax.random.permutation(jax.random.fold_in(rng, 2), count)]


def noise(own_key, shape, deviation, most, split=(), kind=jnp.bfloat16):
    array = deviation * jax.random.normal(own_key, shape, jnp.float32)
    if split:
        array = array * steps_of(own_key, shape, split, -0.22, 0.18)
    return jnp.clip(array, -most, most).astype(kind)


def setup_inputs(seed: int = 0) -> dict:
    key_list = jax.random.split(jax.random.key(seed), 14)
    return {
        "node_features": noise(key_list[0], (NODES, NCOEF, C), 1.0, 6.0, ((0, 32),)),
        "cotangent": noise(key_list[1], (NODES, NCOEF, C), 0.1, 0.59765625, ((0, 32),)),
        "wigner": noise(key_list[2], (WIG, EDGES), 0.4, 2.4, ((1, 32),), jnp.float32),
        "w_zero": noise(key_list[3], ((LMAX + 1) * C, (LMAX + 1) * C), ((LMAX + 1) * C) ** -0.5, 0.1875),
        "w_one_re": noise(key_list[4], (LMAX * C, LMAX * C), (2 * LMAX * C) ** -0.5, 0.15625),
        "w_one_im": noise(key_list[5], (LMAX * C, LMAX * C), (2 * LMAX * C) ** -0.5, 0.15625),
        "w_two_re": noise(key_list[6], ((LMAX - 1) * C, (LMAX - 1) * C), (2 * (LMAX - 1) * C) ** -0.5, 0.15625),
        "w_two_im": noise(key_list[7], ((LMAX - 1) * C, (LMAX - 1) * C), (2 * (LMAX - 1) * C) ** -0.5, 0.15625),
        "w_attn": noise(key_list[8], ((LMAX + 1) * C, H), ((LMAX + 1) * C) ** -0.5, 0.1875),
        "src_slot": place_ends(jax.random.randint(key_list[9], (EDGES,), 0, FETCHED), jax.random.fold_in(key_list[9], 1), 0, FETCHED - 1).astype(jnp.int32),
        "dst_node": place_ends(jax.random.randint(key_list[10], (EDGES,), 0, NODE_DEV), jax.random.fold_in(key_list[10], 1), 0, NODE_DEV - 1).astype(jnp.int32),
        "request": draw_request(jax.random.fold_in(key_list[13], 71), 0),
        "edge_count": uneven(key_list[12], SHARDS, SHARDS * EDGE_DEV * 5 // 8, EDGE_DEV, 2).astype(jnp.int32),
    }


highest_precision = lax.Precision.HIGHEST


def block_offset(degree):
    offset = 0
    for lower in range(degree):
        offset += (2 * min(lower, MMAX) + 1) * (2 * lower + 1)
    return offset


def wigner_block(wigner, degree):
    row_count = 2 * min(degree, MMAX) + 1
    col_count = 2 * degree + 1
    offset = block_offset(degree)
    return wigner[offset:offset + row_count * col_count].reshape(row_count, col_count, wigner.shape[1])


def rotate_blocks(wigner, values):
    result = []
    for degree in range(LMAX + 1):
        block = wigner_block(wigner, degree)
        piece = values[:, degree * degree:(degree + 1) ** 2, :]
        result.append(jnp.einsum("rke,ekc->erc", block, piece, precision=highest_precision))
    return result


def group_orders(blocks):
    order_zero = jnp.stack([blocks[d][:, min(d, MMAX)] for d in range(LMAX + 1)], 1)
    one_plus = jnp.stack([blocks[d][:, min(d, MMAX) + 1] for d in range(1, LMAX + 1)], 1)
    one_minus = jnp.stack([blocks[d][:, min(d, MMAX) - 1] for d in range(1, LMAX + 1)], 1)
    two_plus = jnp.stack([blocks[d][:, min(d, MMAX) + 2] for d in range(2, LMAX + 1)], 1)
    two_minus = jnp.stack([blocks[d][:, min(d, MMAX) - 2] for d in range(2, LMAX + 1)], 1)
    return order_zero, one_plus, one_minus, two_plus, two_minus


def ungroup_orders(order_zero, one_plus, one_minus, two_plus, two_minus):
    blocks = []
    for degree in range(LMAX + 1):
        rows_here = []
        if degree >= 2:
            rows_here.append(two_minus[:, degree - 2])
        if degree >= 1:
            rows_here.append(one_minus[:, degree - 1])
        rows_here.append(order_zero[:, degree])
        if degree >= 1:
            rows_here.append(one_plus[:, degree - 1])
        if degree >= 2:
            rows_here.append(two_plus[:, degree - 2])
        blocks.append(jnp.stack(rows_here, 1))
    return blocks


def flatten_rows(values):
    return values.reshape(values.shape[0], -1)


def product(left, right):
    return jnp.dot(left, right, preferred_element_type=jnp.float32)


def contract_rows(left, right):
    return lax.dot_general(left, right, (((0,), (0,)), ((), ())), preferred_element_type=jnp.float32)


def times_transpose(left, right):
    return lax.dot_general(left, right, (((1,), (1,)), ((), ())), preferred_element_type=jnp.float32)


def edge_backward(source_rows, cot_rows, wigner, live_mask, w_zero, w_one_re, w_one_im, w_two_re, w_two_im, w_attn):
    num_edges = source_rows.shape[0]
    channels = source_rows.shape[2]
    head_count = w_attn.shape[1]
    head_width = channels // head_count
    grouped = group_orders(rotate_blocks(wigner, source_rows.astype(jnp.float32)))
    input_zero, input_one_p, input_one_n, input_two_p, input_two_n = [flatten_rows(member).astype(jnp.bfloat16) for member in grouped]
    output_zero = product(input_zero, w_zero)
    output_one_p = product(input_one_p, w_one_re) - product(input_one_n, w_one_im)
    output_one_n = product(input_one_p, w_one_im) + product(input_one_n, w_one_re)
    output_two_p = product(input_two_p, w_two_re) - product(input_two_n, w_two_im)
    output_two_n = product(input_two_p, w_two_im) + product(input_two_n, w_two_re)
    zero_rounded = output_zero.astype(jnp.bfloat16)
    weighting = jax.nn.sigmoid(product(zero_rounded, w_attn))
    cot_live = cot_rows.astype(jnp.float32) * live_mask[:, None, None]
    back_groups = group_orders(rotate_blocks(wigner, cot_live))
    outputs = (output_zero, output_one_p, output_one_n, output_two_p, output_two_n)
    agreement = jnp.zeros((num_edges, channels), jnp.float32)
    for member, output_part in zip(back_groups, outputs):
        agreement = agreement + jnp.sum(member * output_part.reshape(member.shape), axis=1)
    head_sum = agreement.reshape(num_edges, head_count, head_width).sum(-1)
    logit_grad = (head_sum * weighting * (1.0 - weighting)).astype(jnp.bfloat16)
    spread = jnp.repeat(weighting, head_width, axis=1)[:, None, :]
    back_zero, back_one_p, back_one_n, back_two_p, back_two_n = back_groups
    grad_out_zero = (flatten_rows(back_zero * spread) + times_transpose(logit_grad, w_attn)).astype(jnp.bfloat16)
    grad_out_one_p = flatten_rows(back_one_p * spread).astype(jnp.bfloat16)
    grad_out_one_n = flatten_rows(back_one_n * spread).astype(jnp.bfloat16)
    grad_out_two_p = flatten_rows(back_two_p * spread).astype(jnp.bfloat16)
    grad_out_two_n = flatten_rows(back_two_n * spread).astype(jnp.bfloat16)
    partials = (
        contract_rows(input_zero, grad_out_zero),
        contract_rows(input_one_p, grad_out_one_p) + contract_rows(input_one_n, grad_out_one_n),
        contract_rows(input_one_p, grad_out_one_n) - contract_rows(input_one_n, grad_out_one_p),
        contract_rows(input_two_p, grad_out_two_p) + contract_rows(input_two_n, grad_out_two_n),
        contract_rows(input_two_p, grad_out_two_n) - contract_rows(input_two_n, grad_out_two_p),
        contract_rows(zero_rounded, logit_grad),
    )
    input_grad_zero = times_transpose(grad_out_zero, w_zero)
    input_grad_one_p = times_transpose(grad_out_one_p, w_one_re) + times_transpose(grad_out_one_n, w_one_im)
    input_grad_one_n = times_transpose(grad_out_one_n, w_one_re) - times_transpose(grad_out_one_p, w_one_im)
    input_grad_two_p = times_transpose(grad_out_two_p, w_two_re) + times_transpose(grad_out_two_n, w_two_im)
    input_grad_two_n = times_transpose(grad_out_two_n, w_two_re) - times_transpose(grad_out_two_p, w_two_im)
    blocks = ungroup_orders(
        input_grad_zero.reshape(num_edges, -1, channels),
        input_grad_one_p.reshape(num_edges, -1, channels),
        input_grad_one_n.reshape(num_edges, -1, channels),
        input_grad_two_p.reshape(num_edges, -1, channels),
        input_grad_two_n.reshape(num_edges, -1, channels),
    )
    pieces = []
    for degree in range(LMAX + 1):
        pieces.append(jnp.einsum("rke,erc->ekc", wigner_block(wigner, degree), blocks[degree], precision=highest_precision))
    return jnp.concatenate(pieces, axis=1), partials


def reference(node_features, cotangent, wigner, w_zero, w_one_re, w_one_im, w_two_re, w_two_im, w_attn, src_slot, dst_node, request, edge_count):
    group_nodes = N_GRAPH * NODE_DEV
    owner_base = (jnp.arange(N_GRAPH, dtype=jnp.int32) * NODE_DEV)[:, None]
    weights = (w_zero, w_one_re, w_one_im, w_two_re, w_two_im, w_attn)

    def visit(carry, shard_index):
        node_total, weight_total = carry
        group_index = shard_index // N_GRAPH
        group_rows = lax.dynamic_slice_in_dim(node_features, (group_index * group_nodes).astype(jnp.int32), group_nodes, 0)
        wanted = lax.dynamic_index_in_dim(request, shard_index, 0, keepdims=False)
        local_index = (owner_base + wanted).reshape(-1).astype(jnp.int32)
        first_edge = (shard_index * EDGE_DEV).astype(jnp.int32)
        sources = lax.dynamic_slice_in_dim(src_slot, first_edge, EDGE_DEV, 0)
        targets = lax.dynamic_slice_in_dim(dst_node, first_edge, EDGE_DEV, 0)
        wigner_here = lax.dynamic_slice_in_dim(wigner, first_edge, EDGE_DEV, 1)
        own_cot = lax.dynamic_slice_in_dim(cotangent, (shard_index * NODE_DEV).astype(jnp.int32), NODE_DEV, 0)
        source_rows = jnp.take(group_rows, local_index[sources], axis=0)
        cot_rows = jnp.take(own_cot, targets, axis=0)
        live_mask = (jnp.arange(EDGE_DEV, dtype=jnp.int32) < edge_count[shard_index]).astype(jnp.float32)
        source_grad, partials = edge_backward(source_rows, cot_rows, wigner_here, live_mask, w_zero, w_one_re, w_one_im, w_two_re, w_two_im, w_attn)
        slot_grad = jax.ops.segment_sum(source_grad, sources, num_segments=N_GRAPH * SLOTS).astype(jnp.bfloat16)
        slot_grad = lax.optimization_barrier(slot_grad).astype(jnp.float32)
        node_total = node_total.at[group_index * group_nodes + local_index].add(slot_grad)
        rounded = lax.optimization_barrier(tuple(p.astype(jnp.bfloat16) for p in partials))
        weight_total = tuple(t + r.astype(jnp.float32) for t, r in zip(weight_total, rounded))
        return (node_total, weight_total), None

    start = (jnp.zeros(node_features.shape, jnp.float32), tuple(jnp.zeros(w.shape, jnp.float32) for w in weights))
    (node_total, weight_total), _ = lax.scan(visit, start, jnp.arange(SHARDS, dtype=jnp.int32))
    factor = 1.0 / N_DP
    return (node_total, weight_total[0] * factor, weight_total[1] * factor, weight_total[2] * factor, weight_total[3] * factor, weight_total[4] * factor, weight_total[5] * factor)
```

```python
import functools

import jax
import jax.numpy as jnp
from jax import lax
from jax.experimental import pallas as pl
from jax.experimental.pallas import tpu as pltpu
from jax.sharding import PartitionSpec as P

LMAX = 6
MMAX = 2
NCOEF = (LMAX + 1) ** 2
ORDERS = (0, 1, -1, 2, -2)
MESH = pl.DeviceIdType.MESH
BF = jnp.bfloat16
F32 = jnp.float32
QUARTERS = 4
WIDTH = -(-NCOEF // QUARTERS)
CHUNK = 32


def block_offset(degree):
    offset = 0
    for lower in range(degree):
        offset += (2 * min(lower, MMAX) + 1) * (2 * lower + 1)
    return offset


def entry_index(degree, order, column):
    row = min(degree, MMAX) + order
    return block_offset(degree) + row * (2 * degree + 1) + column


def dot(left, right, dims, precision=None):
    return lax.dot_general(
        left, right, (dims, ((), ())), preferred_element_type=F32, precision=precision
    )


NN = ((1,), (0,))
NT = ((1,), (1,))
TN = ((0,), (0,))


def to_rows(values):
    nodes, coef, ch = values.shape
    padded = jnp.pad(values, ((0, 0), (0, QUARTERS * WIDTH - coef), (0, 0)))
    return (
        padded.reshape(nodes, QUARTERS, WIDTH * ch)
        .transpose(1, 0, 2)
        .reshape(QUARTERS * nodes, WIDTH * ch)
    )


def from_rows(rows, nodes, coef, ch):
    whole = rows.reshape(QUARTERS, nodes, WIDTH * ch).transpose(1, 0, 2)
    return whole.reshape(nodes, QUARTERS * WIDTH, ch)[:, :coef]


def gather_kernel(peers, x_ref, out_ref, send_sem, recv_sem):
    me = lax.axis_index("graph")
    rows = x_ref.shape[0]
    barrier = pltpu.get_barrier_semaphore()
    for d in range(1, peers):
        pl.semaphore_signal(
            barrier, inc=1, device_id={"graph": lax.rem(me + d, peers)}, device_id_type=MESH
        )
    pl.semaphore_wait(barrier, peers - 1)
    mine = pl.ds(pl.multiple_of(me * rows, rows), rows)
    copies = []
    for d in range(1, peers):
        copy = pltpu.make_async_remote_copy(
            src_ref=x_ref,
            dst_ref=out_ref.at[mine],
            send_sem=send_sem.at[d - 1],
            recv_sem=recv_sem.at[d - 1],
            device_id={"graph": lax.rem(me + d, peers)},
            device_id_type=MESH,
        )
        copy.start()
        copies.append(copy)
    out_ref[mine] = x_ref[...]
    for copy in copies:
        copy.wait()


def gather_nodes(x, peers):
    return pl.pallas_call(
        functools.partial(gather_kernel, peers),
        name="gather_nodes",
        out_shape=jax.ShapeDtypeStruct((peers * x.shape[0], x.shape[1]), x.dtype),
        in_specs=[pl.BlockSpec(memory_space=pltpu.VMEM)],
        out_specs=pl.BlockSpec(memory_space=pltpu.VMEM),
        scratch_shapes=[
            pltpu.SemaphoreType.DMA((peers - 1,)),
            pltpu.SemaphoreType.DMA((peers - 1,)),
        ],
        compiler_params=pltpu.CompilerParams(
            collective_id=0, has_side_effects=True, vmem_limit_bytes=24 * 2**20
        ),
    )(x)


def shard_plan(peers, ch, heads_padded):
    plan, at = [], 0
    for which, degrees in enumerate((LMAX + 1, LMAX, LMAX, LMAX - 1, LMAX - 1)):
        rows = degrees * ch // peers
        for cb in range(degrees):
            plan.append((which, cb, at, rows))
            at += rows
    rows = (LMAX + 1) * ch // peers
    plan.append((5, 0, at, rows))
    return plan, at + rows


def compute_kernel(
    peers, nodes, slots, heads, plan, packed,
    g_ref, cot_ref, wig_ref, wz_ref, w1r_ref, w1i_ref, w2r_ref, w2i_ref, wa_ref,
    src_ref, dst_ref, req_ref, count_ref,
    *rest,
):
    if packed:
        (t_ref, n_ref), rest = rest[:2], rest[2:]
    else:
        (tz_ref, t1r_ref, t1i_ref, t2r_ref, t2i_ref, ta_ref, n_ref), rest = rest[:7], rest[7:]
    (srcT, cotT, izT, i1T, i2T, iz, i1, i2, bT, oh_s, igT, sgT, gz, g1, g2, bk) = rest
    ch = 128
    edges = src_ref.shape[1]
    per = QUARTERS * nodes
    k = peers * per

    src = src_ref[...]
    base = jnp.zeros((1, edges), jnp.int32)
    for s in range(peers * slots):
        base = jnp.where(src == s, (s // slots) * per + req_ref[s // slots, s % slots], base)
    iota_k = lax.broadcasted_iota(jnp.int32, (k, edges), 0)
    for q in range(QUARTERS):
        hot = jnp.where(iota_k == base + q * nodes, 1.0, 0.0).astype(BF)
        oh_s[q] = hot
        srcT[pl.ds(q * WIDTH * ch, WIDTH * ch), :] = dot(g_ref[...], hot, TN)
    live = lax.broadcasted_iota(jnp.int32, (1, edges), 1) < count_ref[0]
    target = jnp.where(live, dst_ref[...], -per)
    iota_c = lax.broadcasted_iota(jnp.int32, (per, edges), 0)
    for q in range(QUARTERS):
        hot = jnp.where(iota_c == target + q * nodes, 1.0, 0.0).astype(BF)
        cotT[pl.ds(q * WIDTH * ch, WIDTH * ch), :] = dot(cot_ref[...], hot, TN)

    firsts = {0: 0, 1: LMAX + 1, -1: 2 * LMAX + 1, 2: 3 * LMAX + 1, -2: 4 * LMAX}

    def block_of(degree, order):
        return firsts[order] + degree - abs(order)

    def rotate_step(step, carry):
        at = step * CHUNK
        for degree in range(LMAX + 1):
            reach = min(degree, MMAX)
            for source, is_cot in ((srcT, False), (cotT, True)):
                acc = {}
                for column in range(2 * degree + 1):
                    row0 = (degree * degree + column) * ch
                    value = source[pl.ds(pl.multiple_of(row0 + at, CHUNK), CHUNK), :]
                    for order in range(-reach, reach + 1):
                        index = entry_index(degree, order, column)
                        term = wig_ref[index : index + 1, :] * value
                        acc[order] = acc[order] + term if order in acc else term
                for order in range(-reach, reach + 1):
                    if is_cot:
                        row0 = block_of(degree, order) * ch
                        bT[pl.ds(pl.multiple_of(row0 + at, CHUNK), CHUNK), :] = acc[order]
                        continue
                    row0 = (degree - abs(order)) * ch
                    rows = pl.ds(pl.multiple_of(row0 + at, CHUNK), CHUNK)
                    rounded = acc[order].astype(BF)
                    if order == 0:
                        izT[rows, :] = rounded
                    else:
                        half = 0 if order > 0 else edges
                        held = i1T if abs(order) == 1 else i2T
                        held[rows, half : half + edges] = rounded
        return carry

    lax.fori_loop(0, ch // CHUNK, rotate_step, 0)

    def turn(block):
        return jnp.transpose(block)

    for j in range(LMAX + 1):
        cols = slice(j * ch, (j + 1) * ch)
        iz[:, cols] = turn(izT[cols, :].astype(F32)).astype(BF)
    for j in range(LMAX):
        cols = slice(j * ch, (j + 1) * ch)
        for half in range(2):
            lanes = slice(half * edges, (half + 1) * edges)
            i1[lanes, cols] = turn(i1T[cols, lanes].astype(F32)).astype(BF)
            if j < LMAX - 1:
                i2[lanes, cols] = turn(i2T[cols, lanes].astype(F32)).astype(BF)
    blocks = 5 * LMAX - 1
    for j in range(blocks):
        bk[j] = turn(bT[j * ch : (j + 1) * ch, :])

    out_zero = dot(iz[...], wz_ref[...], NN)
    zero_rounded = out_zero.astype(BF)
    agreement = jnp.zeros((edges, ch), F32)
    for j in range(LMAX + 1):
        agreement = agreement + bk[j] * out_zero[:, j * ch : (j + 1) * ch]
    for order, degrees, held, re_ref, im_ref in (
        (1, LMAX, i1, w1r_ref, w1i_ref),
        (2, LMAX - 1, i2, w2r_ref, w2i_ref),
    ):
        with_re = dot(held[...], re_ref[...], NN)
        with_im = dot(held[...], im_ref[...], NN)
        out_p = with_re[:edges] - with_im[edges:]
        out_n = with_im[:edges] + with_re[edges:]
        for j in range(degrees):
            cols = slice(j * ch, (j + 1) * ch)
            agreement = agreement + bk[firsts[order] + j] * out_p[:, cols]
            agreement = agreement + bk[firsts[-order] + j] * out_n[:, cols]

    wa = wa_ref[...]
    weighting = jax.nn.sigmoid(dot(zero_rounded, wa, NN))
    head_of = lax.broadcasted_iota(jnp.int32, (ch, ch), 0) // (ch // heads)
    member = jnp.where(head_of == lax.broadcasted_iota(jnp.int32, (ch, ch), 1), 1.0, 0.0)
    exact = lax.Precision.HIGHEST
    head_sum = dot(agreement, member, NN, exact)
    logit_grad = (head_sum * weighting * (1.0 - weighting)).astype(BF)
    spread = dot(weighting, member, NT, exact)

    from_logit = dot(logit_grad, wa, NT)
    for j in range(LMAX + 1):
        cols = slice(j * ch, (j + 1) * ch)
        gz[:, cols] = (bk[j] * spread + from_logit[:, cols]).astype(BF)
    for order, degrees, held in ((1, LMAX, g1), (2, LMAX - 1, g2)):
        for j in range(degrees):
            cols = slice(j * ch, (j + 1) * ch)
            plus = (bk[firsts[order] + j] * spread).astype(BF)
            minus = (bk[firsts[-order] + j] * spread).astype(BF)
            held[0:edges, cols] = plus
            held[edges : 2 * edges, cols] = minus
            held[2 * edges : 3 * edges, cols] = -plus

    terms = (
        (0, lambda: dot(izT[...], gz[...], NN)),
        (1, lambda: dot(i1T[...], g1[0 : 2 * edges, :], NN)),
        (2, lambda: dot(i1T[...], g1[edges : 3 * edges, :], NN)),
        (3, lambda: dot(i2T[...], g2[0 : 2 * edges, :], NN)),
        (4, lambda: dot(i2T[...], g2[edges : 3 * edges, :], NN)),
        (5, lambda: dot(zero_rounded, logit_grad, TN)),
    )
    for which, make in terms:
        value = make().astype(BF)
        if not packed:
            (tz_ref, t1r_ref, t1i_ref, t2r_ref, t2i_ref, ta_ref)[which][...] = value
            continue
        for owner, cb, at, rows in plan:
            if owner != which:
                continue
            for g in range(peers):
                t_ref[g, at : at + rows, :] = value[
                    g * rows : (g + 1) * rows, cb * ch : (cb + 1) * ch
                ]
    if packed:
        used = plan[-1][2] + plan[-1][3]
        spare = t_ref.shape[1] - used
        if spare:
            for g in range(peers):
                t_ref[g, used : used + spare, :] = jnp.zeros((spare, ch), BF)

    def put(block, degrees, value):
        igT[block * ch : (block + degrees) * ch, :] = value

    put(0, LMAX + 1, dot(wz_ref[...], gz[...], NT))
    for order, degrees, held, re_ref, im_ref in (
        (1, LMAX, g1, w1r_ref, w1i_ref),
        (2, LMAX - 1, g2, w2r_ref, w2i_ref),
    ):
        both = held[0 : 2 * edges, :]
        with_re = dot(re_ref[...], both, NT)
        with_im = dot(im_ref[...], both, NT)
        put(firsts[order], degrees, with_re[:, :edges] + with_im[:, edges:])
        put(firsts[-order], degrees, with_re[:, edges:] - with_im[:, :edges])

    def unrotate_step(step, carry):
        at = step * CHUNK
        for degree in range(LMAX + 1):
            reach = min(degree, MMAX)
            held = {}
            for order in range(-reach, reach + 1):
                row0 = block_of(degree, order) * ch
                held[order] = igT[pl.ds(pl.multiple_of(row0 + at, CHUNK), CHUNK), :]
            for column in range(2 * degree + 1):
                total = None
                for order in range(-reach, reach + 1):
                    index = entry_index(degree, order, column)
                    term = wig_ref[index : index + 1, :] * held[order]
                    total = term if total is None else total + term
                row0 = (degree * degree + column) * ch
                sgT[pl.ds(pl.multiple_of(row0 + at, CHUNK), CHUNK), :] = total.astype(BF)
        return carry

    lax.fori_loop(0, ch // CHUNK, unrotate_step, 0)
    tail = QUARTERS * WIDTH - NCOEF
    if tail:
        sgT[NCOEF * ch : (NCOEF + tail) * ch, :] = jnp.zeros((tail * ch, edges), BF)
    total = None
    for q in range(QUARTERS):
        part = dot(oh_s[q], sgT[q * WIDTH * ch : (q + 1) * WIDTH * ch, :], NT)
        total = part if total is None else total + part
    n_ref[...] = total.astype(BF)


def compute(peers, nodes, slots, heads, plan, rows_padded, packed, *args):
    ch = 128
    edges = args[9].shape[1]
    wide, mid, low = (LMAX + 1) * ch, LMAX * ch, (LMAX - 1) * ch
    blocks = 5 * LMAX - 1
    k = peers * QUARTERS * nodes
    if packed:
        outs = [jax.ShapeDtypeStruct((peers, rows_padded, ch), BF)]
    else:
        outs = [
            jax.ShapeDtypeStruct(shape, BF)
            for shape in ((wide, wide), (mid, mid), (mid, mid), (low, low), (low, low), (wide, ch))
        ]
    outs.append(jax.ShapeDtypeStruct((k, WIDTH * ch), BF))
    vmem = pl.BlockSpec(memory_space=pltpu.VMEM)
    smem = pl.BlockSpec(memory_space=pltpu.SMEM)
    coefs = QUARTERS * WIDTH * ch
    return pl.pallas_call(
        functools.partial(compute_kernel, peers, nodes, slots, heads, plan, packed),
        name="edge_backward",
        out_shape=outs,
        in_specs=[vmem] * 11 + [smem] * 2,
        out_specs=[vmem] * len(outs),
        scratch_shapes=[
            pltpu.VMEM((coefs, edges), F32),
            pltpu.VMEM((coefs, edges), F32),
            pltpu.VMEM((wide, edges), BF),
            pltpu.VMEM((mid, 2 * edges), BF),
            pltpu.VMEM((low, 2 * edges), BF),
            pltpu.VMEM((edges, wide), BF),
            pltpu.VMEM((2 * edges, mid), BF),
            pltpu.VMEM((2 * edges, low), BF),
            pltpu.VMEM((blocks * ch, edges), F32),
            pltpu.VMEM((QUARTERS, k, edges), BF),
            pltpu.VMEM((blocks * ch, edges), F32),
            pltpu.VMEM((coefs, edges), BF),
            pltpu.VMEM((edges, wide), BF),
            pltpu.VMEM((3 * edges, mid), BF),
            pltpu.VMEM((3 * edges, low), BF),
            pltpu.VMEM((blocks, edges, ch), F32),
        ],
        compiler_params=pltpu.CompilerParams(vmem_limit_bytes=56 * 2**20),
    )(*args)


def reduce_kernel(
    ny, nx, nz, h,
    t_ref, n_ref, out_ref, node_ref,
    r0, r1y, r1x, r2x, r2y, r3, mine, gathered, nodes_in, send_sem, recv_sem,
):
    dp = lax.axis_index("dp")
    gi = lax.axis_index("graph")
    core, y = lax.rem(dp, 2), dp // 2
    x, z = lax.rem(gi, nx), gi // nx
    peers = nx * nz
    ndp = 2 * ny
    chn = 128

    def at_y(v):
        return {"dp": v * 2 + core}

    def at_x(v):
        return {"graph": z * nx + v}

    def at_z(v):
        return {"graph": v * nx + x}

    barrier = pltpu.get_barrier_semaphore()
    for d in range(1, ndp):
        pl.semaphore_signal(
            barrier, inc=1, device_id={"dp": lax.rem(dp + d, ndp)}, device_id_type=MESH
        )
    for d in range(1, peers):
        pl.semaphore_signal(
            barrier, inc=1, device_id={"graph": lax.rem(gi + d, peers)}, device_id_type=MESH
        )
    pl.semaphore_wait(barrier, ndp - 1 + peers - 1)

    used = [0]

    def send(source, target, device):
        i = used[0]
        used[0] += 1
        copy = pltpu.make_async_remote_copy(
            src_ref=source, dst_ref=target, send_sem=send_sem.at[i], recv_sem=recv_sem.at[i],
            device_id=device, device_id_type=MESH,
        )
        copy.start()
        return copy

    def span(index, size):
        return pl.ds(pl.multiple_of(index * size, 16), size)

    yh = ny * h
    started = []
    first = []
    for part in range(2):
        first.append(
            send(t_ref.at[:, span(part * 2 + (1 - core), yh)], r0.at[part], {"dp": y * 2 + 1 - core})
        )
    node_copies = []
    rows = node_ref.shape[0]
    for d in range(1, peers):
        to = lax.rem(gi + d, peers)
        node_copies.append(send(n_ref.at[span(to, rows)], nodes_in.at[d - 1], {"graph": to}))

    def add_first(part):
        first[part].wait_recv()
        own = span(part * 2 + core, yh)

        def step(g, carry):
            r0[part, g] = (r0[part, g].astype(F32) + t_ref[g, own].astype(F32)).astype(BF)
            return carry

        lax.fori_loop(0, peers, step, 0)

    add_first(0)
    along_y = []
    for d in range(1, ny):
        to = lax.rem(y + d, ny)
        along_y.append(send(r0.at[0, :, span(to, h)], r1y.at[d - 1], at_y(to)))
    add_first(1)
    along_x = []
    for d in range(1, nx):
        to = lax.rem(x + d, nx)
        along_x.append(
            [send(r0.at[1, zz * nx + to], r1x.at[d - 1, zz], at_x(to)) for zz in range(nz)]
        )

    for copy in along_y:
        copy.wait_recv()

    def sum_y(g, carry):
        total = r0[0, g, span(y, h)].astype(F32)
        for d in range(1, ny):
            total = total + r1y[d - 1, g].astype(F32)
        r1y[ny - 1, g] = total.astype(BF)
        return carry

    lax.fori_loop(0, peers, sum_y, 0)
    second_x = []
    for d in range(1, nx):
        to = lax.rem(x + d, nx)
        second_x.append(
            [send(r1y.at[ny - 1, zz * nx + to], r2x.at[d - 1, zz], at_x(to)) for zz in range(nz)]
        )

    for group in along_x:
        for copy in group:
            copy.wait_recv()

    def sum_x(zz, carry):
        total = r0[1, zz * nx + x].astype(F32)
        for d in range(1, nx):
            total = total + r1x[d - 1, zz].astype(F32)
        r1x[nx - 1, zz] = total.astype(BF)
        return carry

    lax.fori_loop(0, nz, sum_x, 0)
    second_y = []
    for d in range(1, ny):
        to = lax.rem(y + d, ny)
        second_y.append(send(r1x.at[nx - 1, :, span(to, h)], r2y.at[d - 1], at_y(to)))

    for group in second_x:
        for copy in group:
            copy.wait_recv()

    def sum_2x(zz, carry):
        total = r1y[ny - 1, zz * nx + x].astype(F32)
        for d in range(1, nx):
            total = total + r2x[d - 1, zz].astype(F32)
        r2x[nx - 1, zz] = total.astype(BF)
        return carry

    lax.fori_loop(0, nz, sum_2x, 0)
    third = [[], []]
    for d in range(1, nz):
        to = lax.rem(z + d, nz)
        third[0].append(send(r2x.at[nx - 1, to], r3.at[0, d - 1], at_z(to)))
    for copy in second_y:
        copy.wait_recv()

    def sum_2y(zz, carry):
        total = r1x[nx - 1, zz, span(y, h)].astype(F32)
        for d in range(1, ny):
            total = total + r2y[d - 1, zz].astype(F32)
        r2y[ny - 1, zz] = total.astype(BF)
        return carry

    lax.fori_loop(0, nz, sum_2y, 0)
    for d in range(1, nz):
        to = lax.rem(z + d, nz)
        third[1].append(send(r2y.at[ny - 1, to], r3.at[1, d - 1], at_z(to)))

    total = n_ref[span(gi, rows)].astype(F32)
    for d in range(1, peers):
        node_copies[d - 1].wait_recv()
        total = total + nodes_in[d - 1].astype(F32)
    node_ref[...] = total

    last = []
    for part in range(2):
        for copy in third[part]:
            copy.wait_recv()
        total = (r2x[nx - 1, z] if part == 0 else r2y[ny - 1, z]).astype(F32)
        for d in range(1, nz):
            total = total + r3[part, d - 1].astype(F32)
        mine[part] = (total * (1.0 / ndp)).astype(BF)
        for d in range(1, ndp):
            to = lax.rem(dp + d, ndp)
            last.append(send(mine.at[part], gathered.at[part, d - 1], {"dp": to}))
    for part in range(2):
        out_ref[span(part * ndp + core * ny + y, h)] = mine[part]
    for i, copy in enumerate(last):
        part, d = i // (ndp - 1), i % (ndp - 1) + 1
        copy.wait_recv()
        who = lax.rem(dp + ndp - d, ndp)
        out_ref[span(part * ndp + lax.rem(who, 2) * ny + who // 2, h)] = gathered[part, d - 1]
    for copy in first + node_copies + along_y + second_y + third[0] + third[1] + last:
        copy.wait_send()
    for group in along_x + second_x:
        for copy in group:
            copy.wait_send()


def reduce_all(terms, node_terms, ny, nx, nz):
    peers, rows_padded, ch = terms.shape
    ndp = 2 * ny
    h = rows_padded // (2 * ndp)
    rows = node_terms.shape[0] // peers
    sends = 2 + (peers - 1) + 2 * (ny - 1) + 2 * (nx - 1) * nz + 2 * (nz - 1) + 2 * (ndp - 1)
    vmem = pl.BlockSpec(memory_space=pltpu.VMEM)
    return pl.pallas_call(
        functools.partial(reduce_kernel, ny, nx, nz, h),
        name="reduce_all",
        out_shape=[
            jax.ShapeDtypeStruct((rows_padded, ch), BF),
            jax.ShapeDtypeStruct((rows, node_terms.shape[1]), F32),
        ],
        in_specs=[vmem] * 2,
        out_specs=[vmem] * 2,
        scratch_shapes=[
            pltpu.VMEM((2, peers, ny * h, ch), BF),
            pltpu.VMEM((ny, peers, h, ch), BF),
            pltpu.VMEM((nx, nz, ny * h, ch), BF),
            pltpu.VMEM((nx, nz, h, ch), BF),
            pltpu.VMEM((ny, nz, h, ch), BF),
            pltpu.VMEM((2, max(nz - 1, 1), h, ch), BF),
            pltpu.VMEM((2, h, ch), BF),
            pltpu.VMEM((2, ndp - 1, h, ch), BF),
            pltpu.VMEM((peers - 1, rows, node_terms.shape[1]), BF),
            pltpu.SemaphoreType.DMA((sends,)),
            pltpu.SemaphoreType.DMA((sends,)),
        ],
        compiler_params=pltpu.CompilerParams(
            collective_id=1, has_side_effects=True, vmem_limit_bytes=48 * 2**20
        ),
    )(terms, node_terms)


def per_device(
    node_features, cotangent, wigner, w_zero, w_one_re, w_one_im, w_two_re, w_two_im, w_attn,
    src_slot, dst_node, request, edge_count,
):
    peers = lax.axis_size("graph")
    ndp = lax.axis_size("dp")
    ny = ndp // 2
    nx = ny
    nz = peers // nx
    nodes, coef, ch = node_features.shape
    heads = w_attn.shape[1]
    plan, used = shard_plan(peers, ch, ch)
    unit = 16 * 2 * ndp
    rows_padded = -(-used // unit) * unit
    packed = all(rows % 16 == 0 for _, _, _, rows in plan)

    everyone = gather_nodes(to_rows(node_features), peers)
    results = compute(
        peers, nodes, request.shape[2], heads, plan, rows_padded, packed,
        everyone, to_rows(cotangent), wigner, w_zero, w_one_re, w_one_im, w_two_re, w_two_im,
        jnp.pad(w_attn, ((0, 0), (0, ch - heads))),
        src_slot[None, :], dst_node[None, :], request[0], edge_count,
    )
    node_terms = results[-1]
    if packed:
        terms = results[0]
    else:
        pieces = [
            results[which].reshape(peers, rows, -1)[:, :, cb * ch : (cb + 1) * ch]
            for which, cb, _, rows in plan
        ]
        pieces.append(jnp.zeros((peers, rows_padded - used, ch), BF))
        terms = jnp.concatenate(pieces, axis=1)
    shard, node_rows = reduce_all(terms, node_terms, ny, nx, nz)
    node_grad = from_rows(node_rows, nodes, coef, ch)
    outs = []
    for which in range(5):
        mine = [p for p in plan if p[0] == which]
        at, rows = mine[0][2], mine[0][3]
        block = shard[at : at + rows * len(mine)].reshape(len(mine), rows, ch)
        outs.append(block.transpose(1, 0, 2).reshape(rows, -1).astype(F32))
    _, _, at, rows = plan[-1]
    outs.append(shard[at : at + rows, :heads].astype(F32))
    return (node_grad, *outs)


def solution(mesh):
    both = ("dp", "graph")
    in_specs = (
        P(both, None, None), P(both, None, None), P(None, both),
        P(), P(), P(), P(), P(), P(),
        P(both), P(both), P(both, None, None), P(both),
    )
    out_specs = (P(both, None, None),) + (P("graph", None),) * 6
    return jax.shard_map(
        per_device, mesh=mesh, in_specs=in_specs, out_specs=out_specs, check_vma=False
    )
```

```python
import functools

import jax
import jax.numpy as jnp
from jax import lax
from jax.experimental import pallas as pl
from jax.experimental.pallas import tpu as pltpu
from jax.sharding import PartitionSpec as P

LMAX = 6
MMAX = 2
NCOEF = (LMAX + 1) ** 2
ORDERS = (0, 1, -1, 2, -2)
MESH = pl.DeviceIdType.MESH
BF = jnp.bfloat16
F32 = jnp.float32
QUARTERS = 4
WIDTH = -(-NCOEF // QUARTERS)
CHUNK = 32
PARTS = 4


def block_offset(degree):
    offset = 0
    for lower in range(degree):
        offset += (2 * min(lower, MMAX) + 1) * (2 * lower + 1)
    return offset


def entry_index(degree, order, column):
    row = min(degree, MMAX) + order
    return block_offset(degree) + row * (2 * degree + 1) + column


def dot(left, right, dims, precision=None):
    return lax.dot_general(
        left, right, (dims, ((), ())), preferred_element_type=F32, precision=precision
    )


NN = ((1,), (0,))
NT = ((1,), (1,))
TN = ((0,), (0,))


def to_rows(values):
    nodes, coef, ch = values.shape
    padded = jnp.pad(values, ((0, 0), (0, QUARTERS * WIDTH - coef), (0, 0)))
    return (
        padded.reshape(nodes, QUARTERS, WIDTH * ch)
        .transpose(1, 0, 2)
        .reshape(QUARTERS * nodes, WIDTH * ch)
    )


def from_rows(rows, nodes, coef, ch):
    whole = rows.reshape(QUARTERS, nodes, WIDTH * ch).transpose(1, 0, 2)
    return whole.reshape(nodes, QUARTERS * WIDTH, ch)[:, :coef]


def gather_kernel(nx, nz, x_ref, out_ref, send_sem, recv_sem):
    me = lax.axis_index("graph")
    x, z = lax.rem(me, nx), me // nx
    rows = x_ref.shape[0]
    along_x = [z * nx + lax.rem(x + d, nx) for d in range(1, nx)]
    along_z = [lax.rem(z + d, nz) * nx + x for d in range(1, nz)]
    barrier = pltpu.get_barrier_semaphore()
    for to in along_x + along_z:
        pl.semaphore_signal(barrier, inc=1, device_id={"graph": to}, device_id_type=MESH)
    pl.semaphore_wait(barrier, nx - 1 + nz - 1)

    def block(index):
        return out_ref.at[pl.ds(pl.multiple_of(index * rows, rows), rows)]

    copies = []

    def send(source, index, to):
        i = len(copies)
        copy = pltpu.make_async_remote_copy(
            src_ref=source, dst_ref=block(index), send_sem=send_sem.at[i],
            recv_sem=recv_sem.at[i], device_id={"graph": to}, device_id_type=MESH,
        )
        copy.start()
        copies.append(copy)
        return copy

    over_z = [send(x_ref, me, to) for to in along_z]
    for to in along_x:
        send(x_ref, me, to)
    out_ref[pl.ds(pl.multiple_of(me * rows, rows), rows)] = x_ref[...]
    for d in range(1, nz):
        over_z[d - 1].wait_recv()
        came = lax.rem(z + nz - d, nz) * nx + x
        for to in along_x:
            send(block(came), came, to)
    for i, copy in enumerate(copies):
        copy.wait_send()
        if i >= nz - 1:
            copy.wait_recv()


def gather_nodes(x, nx, nz):
    sends = nz - 1 + (nx - 1) * nz
    return pl.pallas_call(
        functools.partial(gather_kernel, nx, nz),
        name="gather_nodes",
        out_shape=jax.ShapeDtypeStruct((nx * nz * x.shape[0], x.shape[1]), x.dtype),
        in_specs=[pl.BlockSpec(memory_space=pltpu.VMEM)],
        out_specs=pl.BlockSpec(memory_space=pltpu.VMEM),
        scratch_shapes=[
            pltpu.SemaphoreType.DMA((sends,)),
            pltpu.SemaphoreType.DMA((sends,)),
        ],
        compiler_params=pltpu.CompilerParams(
            collective_id=0, has_side_effects=True, vmem_limit_bytes=24 * 2**20
        ),
    )(x)


def shard_plan(peers, ch, heads_padded):
    plan, at = [], 0
    for which, degrees in enumerate((LMAX + 1, LMAX, LMAX, LMAX - 1, LMAX - 1)):
        rows = degrees * ch // peers
        for cb in range(degrees):
            plan.append((which, cb, at, rows))
            at += rows
    rows = (LMAX + 1) * ch // peers // 2
    plan.append((5, 0, at, rows))
    return plan, at + rows


def compute_kernel(
    peers, nodes, slots, heads, plan, packed,
    g_ref, cot_ref, wig_ref, wz_ref, w1r_ref, w1i_ref, w2r_ref, w2i_ref, wa_ref,
    src_ref, dst_ref, req_ref, count_ref,
    *rest,
):
    if packed:
        (t_ref, n_ref), rest = rest[:2], rest[2:]
    else:
        (tz_ref, t1r_ref, t1i_ref, t2r_ref, t2i_ref, ta_ref, n_ref), rest = rest[:7], rest[7:]
    (srcT, cotT, izT, i1T, i2T, iz, i1, i2, bT, oh_s, igT, sgT, gz, g1, g2, bk) = rest
    ch = 128
    edges = src_ref.shape[1]
    per = QUARTERS * nodes
    k = peers * per

    src = src_ref[...]
    base = jnp.zeros((1, edges), jnp.int32)
    for s in range(peers * slots):
        base = jnp.where(src == s, (s // slots) * per + req_ref[s // slots, s % slots], base)
    iota_k = lax.broadcasted_iota(jnp.int32, (k, edges), 0)
    for q in range(QUARTERS):
        hot = jnp.where(iota_k == base + q * nodes, 1.0, 0.0).astype(BF)
        oh_s[q] = hot
        srcT[pl.ds(q * WIDTH * ch, WIDTH * ch), :] = dot(g_ref[...], hot, TN)
    live = lax.broadcasted_iota(jnp.int32, (1, edges), 1) < count_ref[0]
    target = jnp.where(live, dst_ref[...], -per)
    iota_c = lax.broadcasted_iota(jnp.int32, (per, edges), 0)
    for q in range(QUARTERS):
        hot = jnp.where(iota_c == target + q * nodes, 1.0, 0.0).astype(BF)
        cotT[pl.ds(q * WIDTH * ch, WIDTH * ch), :] = dot(cot_ref[...], hot, TN)

    firsts = {0: 0, 1: LMAX + 1, -1: 2 * LMAX + 1, 2: 3 * LMAX + 1, -2: 4 * LMAX}

    def block_of(degree, order):
        return firsts[order] + degree - abs(order)

    def rotate_step(step, carry):
        at = step * CHUNK
        for degree in range(LMAX + 1):
            reach = min(degree, MMAX)
            for source, is_cot in ((srcT, False), (cotT, True)):
                acc = {}
                for column in range(2 * degree + 1):
                    row0 = (degree * degree + column) * ch
                    value = source[pl.ds(pl.multiple_of(row0 + at, CHUNK), CHUNK), :]
                    for order in range(-reach, reach + 1):
                        index = entry_index(degree, order, column)
                        term = wig_ref[index : index + 1, :] * value
                        acc[order] = acc[order] + term if order in acc else term
                for order in range(-reach, reach + 1):
                    if is_cot:
                        row0 = block_of(degree, order) * ch
                        bT[pl.ds(pl.multiple_of(row0 + at, CHUNK), CHUNK), :] = acc[order]
                        continue
                    row0 = (degree - abs(order)) * ch
                    rows = pl.ds(pl.multiple_of(row0 + at, CHUNK), CHUNK)
                    rounded = acc[order].astype(BF)
                    if order == 0:
                        izT[rows, :] = rounded
                    else:
                        half = 0 if order > 0 else edges
                        held = i1T if abs(order) == 1 else i2T
                        held[rows, half : half + edges] = rounded
        return carry

    lax.fori_loop(0, ch // CHUNK, rotate_step, 0)

    def turn(block):
        return jnp.transpose(block)

    for j in range(LMAX + 1):
        cols = slice(j * ch, (j + 1) * ch)
        iz[:, cols] = turn(izT[cols, :].astype(F32)).astype(BF)
    for j in range(LMAX):
        cols = slice(j * ch, (j + 1) * ch)
        for half in range(2):
            lanes = slice(half * edges, (half + 1) * edges)
            i1[lanes, cols] = turn(i1T[cols, lanes].astype(F32)).astype(BF)
            if j < LMAX - 1:
                i2[lanes, cols] = turn(i2T[cols, lanes].astype(F32)).astype(BF)
    blocks = 5 * LMAX - 1
    for j in range(blocks):
        bk[j] = turn(bT[j * ch : (j + 1) * ch, :])

    out_zero = dot(iz[...], wz_ref[...], NN)
    zero_rounded = out_zero.astype(BF)
    agreement = jnp.zeros((edges, ch), F32)
    for j in range(LMAX + 1):
        agreement = agreement + bk[j] * out_zero[:, j * ch : (j + 1) * ch]
    for order, degrees, held, re_ref, im_ref in (
        (1, LMAX, i1, w1r_ref, w1i_ref),
        (2, LMAX - 1, i2, w2r_ref, w2i_ref),
    ):
        with_re = dot(held[...], re_ref[...], NN)
        with_im = dot(held[...], im_ref[...], NN)
        out_p = with_re[:edges] - with_im[edges:]
        out_n = with_im[:edges] + with_re[edges:]
        for j in range(degrees):
            cols = slice(j * ch, (j + 1) * ch)
            agreement = agreement + bk[firsts[order] + j] * out_p[:, cols]
            agreement = agreement + bk[firsts[-order] + j] * out_n[:, cols]

    wa = wa_ref[...]
    weighting = jax.nn.sigmoid(dot(zero_rounded, wa, NN))
    head_of = lax.broadcasted_iota(jnp.int32, (ch, ch), 0) // (ch // heads)
    member = jnp.where(head_of == lax.broadcasted_iota(jnp.int32, (ch, ch), 1), 1.0, 0.0)
    exact = lax.Precision.HIGHEST
    head_sum = dot(agreement, member, NN, exact)
    logit_grad = (head_sum * weighting * (1.0 - weighting)).astype(BF)
    spread = dot(weighting, member, NT, exact)

    from_logit = dot(logit_grad, wa, NT)
    for j in range(LMAX + 1):
        cols = slice(j * ch, (j + 1) * ch)
        gz[:, cols] = (bk[j] * spread + from_logit[:, cols]).astype(BF)
    for order, degrees, held in ((1, LMAX, g1), (2, LMAX - 1, g2)):
        for j in range(degrees):
            cols = slice(j * ch, (j + 1) * ch)
            plus = (bk[firsts[order] + j] * spread).astype(BF)
            minus = (bk[firsts[-order] + j] * spread).astype(BF)
            held[0:edges, cols] = plus
            held[edges : 2 * edges, cols] = minus
            held[2 * edges : 3 * edges, cols] = -plus

    terms = (
        (0, lambda: dot(izT[...], gz[...], NN)),
        (1, lambda: dot(i1T[...], g1[0 : 2 * edges, :], NN)),
        (2, lambda: dot(i1T[...], g1[edges : 3 * edges, :], NN)),
        (3, lambda: dot(i2T[...], g2[0 : 2 * edges, :], NN)),
        (4, lambda: dot(i2T[...], g2[edges : 3 * edges, :], NN)),
        (5, lambda: dot(zero_rounded, logit_grad, TN)),
    )
    for which, make in terms:
        value = make()
        if which == 5:
            value = value.reshape(peers, 2, -1, ch)
            value = value[:, 0] + pltpu.roll(value[:, 1].reshape(-1, ch), heads, 1).reshape(
                peers, -1, ch
            )
            if packed:
                at, rows = plan[-1][2:]
                spare = t_ref.shape[1] - at - rows
                if spare:
                    value = jnp.concatenate([value, jnp.zeros((peers, spare, ch), F32)], 1)
                t_ref[:, at:, :] = value.astype(BF)
                continue
            value = value.reshape(-1, ch)
        value = value.astype(BF)
        if not packed:
            (tz_ref, t1r_ref, t1i_ref, t2r_ref, t2i_ref, ta_ref)[which][...] = value
            continue
        for owner, cb, at, rows in plan:
            if owner != which:
                continue
            for g in range(peers):
                t_ref[g, at : at + rows, :] = value[
                    g * rows : (g + 1) * rows, cb * ch : (cb + 1) * ch
                ]
    def put(block, degrees, value):
        igT[block * ch : (block + degrees) * ch, :] = value

    put(0, LMAX + 1, dot(wz_ref[...], gz[...], NT))
    for order, degrees, held, re_ref, im_ref in (
        (1, LMAX, g1, w1r_ref, w1i_ref),
        (2, LMAX - 1, g2, w2r_ref, w2i_ref),
    ):
        both = held[0 : 2 * edges, :]
        with_re = dot(re_ref[...], both, NT)
        with_im = dot(im_ref[...], both, NT)
        put(firsts[order], degrees, with_re[:, :edges] + with_im[:, edges:])
        put(firsts[-order], degrees, with_re[:, edges:] - with_im[:, :edges])

    def unrotate_step(step, carry):
        at = step * CHUNK
        for degree in range(LMAX + 1):
            reach = min(degree, MMAX)
            held = {}
            for order in range(-reach, reach + 1):
                row0 = block_of(degree, order) * ch
                held[order] = igT[pl.ds(pl.multiple_of(row0 + at, CHUNK), CHUNK), :]
            for column in range(2 * degree + 1):
                total = None
                for order in range(-reach, reach + 1):
                    index = entry_index(degree, order, column)
                    term = wig_ref[index : index + 1, :] * held[order]
                    total = term if total is None else total + term
                row0 = (degree * degree + column) * ch
                sgT[pl.ds(pl.multiple_of(row0 + at, CHUNK), CHUNK), :] = total.astype(BF)
        return carry

    lax.fori_loop(0, ch // CHUNK, unrotate_step, 0)
    tail = QUARTERS * WIDTH - NCOEF
    if tail:
        sgT[NCOEF * ch : (NCOEF + tail) * ch, :] = jnp.zeros((tail * ch, edges), BF)
    total = None
    for q in range(QUARTERS):
        part = dot(oh_s[q], sgT[q * WIDTH * ch : (q + 1) * WIDTH * ch, :], NT)
        total = part if total is None else total + part
    n_ref[...] = total.astype(BF)


def compute(peers, nodes, slots, heads, plan, rows_padded, packed, *args):
    ch = 128
    edges = args[9].shape[1]
    wide, mid, low = (LMAX + 1) * ch, LMAX * ch, (LMAX - 1) * ch
    blocks = 5 * LMAX - 1
    k = peers * QUARTERS * nodes
    if packed:
        outs = [jax.ShapeDtypeStruct((peers, rows_padded, ch), BF)]
    else:
        outs = [
            jax.ShapeDtypeStruct(shape, BF)
            for shape in ((wide, wide), (mid, mid), (mid, mid), (low, low), (low, low), (wide // 2, ch))
        ]
    outs.append(jax.ShapeDtypeStruct((k, WIDTH * ch), BF))
    vmem = pl.BlockSpec(memory_space=pltpu.VMEM)
    smem = pl.BlockSpec(memory_space=pltpu.SMEM)
    coefs = QUARTERS * WIDTH * ch
    return pl.pallas_call(
        functools.partial(compute_kernel, peers, nodes, slots, heads, plan, packed),
        name="edge_backward",
        out_shape=outs,
        in_specs=[vmem] * 11 + [smem] * 2,
        out_specs=[vmem] * len(outs),
        scratch_shapes=[
            pltpu.VMEM((coefs, edges), F32),
            pltpu.VMEM((coefs, edges), F32),
            pltpu.VMEM((wide, edges), BF),
            pltpu.VMEM((mid, 2 * edges), BF),
            pltpu.VMEM((low, 2 * edges), BF),
            pltpu.VMEM((edges, wide), BF),
            pltpu.VMEM((2 * edges, mid), BF),
            pltpu.VMEM((2 * edges, low), BF),
            pltpu.VMEM((blocks * ch, edges), F32),
            pltpu.VMEM((QUARTERS, k, edges), BF),
            pltpu.VMEM((blocks * ch, edges), F32),
            pltpu.VMEM((coefs, edges), BF),
            pltpu.VMEM((edges, wide), BF),
            pltpu.VMEM((3 * edges, mid), BF),
            pltpu.VMEM((3 * edges, low), BF),
            pltpu.VMEM((blocks, edges, ch), F32),
        ],
        compiler_params=pltpu.CompilerParams(vmem_limit_bytes=56 * 2**20),
    )(*args)


def reduce_kernel(
    ny, nx, nz, h,
    t_ref, n_ref, out_ref, node_ref,
    own, r0, r1y, r1x, r2x, r2y, r3, nodes_in, send_sem, recv_sem, own_sem,
):
    dp = lax.axis_index("dp")
    gi = lax.axis_index("graph")
    core, y = lax.rem(dp, 2), dp // 2
    x, z = lax.rem(gi, nx), gi // nx
    peers = nx * nz
    ndp = 2 * ny
    yh = ny * h

    def at_y(v):
        return {"dp": v * 2 + core}

    def at_x(v):
        return {"graph": z * nx + v}

    def at_z(v):
        return {"graph": v * nx + x}

    other_core = {"dp": y * 2 + 1 - core}

    def span(index, size):
        return pl.ds(pl.multiple_of(index * size, 16), size)

    locals_ = []
    for part in range(PARTS):
        copy = pltpu.make_async_copy(
            t_ref.at[:, :, span(part * 2 + core, yh)], own.at[part], own_sem.at[part]
        )
        copy.start()
        locals_.append(copy)

    barrier = pltpu.get_barrier_semaphore()
    for d in range(1, ndp):
        pl.semaphore_signal(
            barrier, inc=1, device_id={"dp": lax.rem(dp + d, ndp)}, device_id_type=MESH
        )
    for d in range(1, peers):
        pl.semaphore_signal(
            barrier, inc=1, device_id={"graph": lax.rem(gi + d, peers)}, device_id_type=MESH
        )
    pl.semaphore_wait(barrier, ndp - 1 + peers - 1)

    sent = []

    def send(source, target, device):
        i = len(sent)
        copy = pltpu.make_async_remote_copy(
            src_ref=source, dst_ref=target, send_sem=send_sem.at[i], recv_sem=recv_sem.at[i],
            device_id=device, device_id_type=MESH,
        )
        copy.start()
        sent.append(copy)
        return copy

    def arrive(copies):
        for copy in copies:
            copy.wait_recv()

    def offsets(me, n):
        return [(d - 1, lax.rem(me + d, n)) for d in range(1, n)]

    def sum_over_z(target, sources):
        def step(zz, carry):
            total = None
            for source in sources:
                value = source(zz).astype(F32)
                total = value if total is None else total + value
            target[zz] = total.astype(BF)
            return carry

        lax.fori_loop(0, nz, step, 0)

    parts = range(PARTS)
    zero = [
        send(t_ref.at[:, :, span(part * 2 + (1 - core), yh)], r0.at[part], other_core)
        for part in parts
    ]
    rows = node_ref.shape[0]
    node_copies = []
    for slot, to in offsets(gi, peers):
        node_copies.append(send(n_ref.at[span(to, rows)], nodes_in.at[slot], {"graph": to}))

    first = []
    for part in parts:
        i = part // 2
        locals_[part].wait()
        zero[part].wait_recv()
        sum_over_z(
            r0.at[part],
            [lambda zz, part=part: own[part, zz], lambda zz, part=part: r0[part, zz]],
        )
        if part % 2 == 0:
            first.append(
                [send(r0.at[part, :, :, span(to, h)], r1y.at[i, slot], at_y(to))
                 for slot, to in offsets(y, ny)]
            )
        else:
            first.append(
                [send(r0.at[part, :, to], r1x.at[i, slot], at_x(to))
                 for slot, to in offsets(x, nx)]
            )

    second = []
    for part in parts:
        i = part // 2
        arrive(first[part])
        if part % 2 == 0:
            sum_over_z(
                r1y.at[i, ny - 1],
                [lambda zz, part=part: r0[part, zz, :, span(y, h)]]
                + [lambda zz, i=i, d=d: r1y[i, d, zz] for d in range(ny - 1)],
            )
            second.append(
                [send(r1y.at[i, ny - 1, :, to], r2x.at[i, slot], at_x(to))
                 for slot, to in offsets(x, nx)]
            )
        else:
            sum_over_z(
                r1x.at[i, nx - 1],
                [lambda zz, part=part: r0[part, zz, x]]
                + [lambda zz, i=i, d=d: r1x[i, d, zz] for d in range(nx - 1)],
            )
            second.append(
                [send(r1x.at[i, nx - 1, :, span(to, h)], r2y.at[i, slot], at_y(to))
                 for slot, to in offsets(y, ny)]
            )

    third = []
    for part in parts:
        i = part // 2
        arrive(second[part])
        if part % 2 == 0:
            held = r2x.at[i, nx - 1]
            sum_over_z(
                held,
                [lambda zz, i=i: r1y[i, ny - 1, zz, x]]
                + [lambda zz, i=i, d=d: r2x[i, d, zz] for d in range(nx - 1)],
            )
        else:
            held = r2y.at[i, ny - 1]
            sum_over_z(
                held,
                [lambda zz, i=i: r1x[i, nx - 1, zz, span(y, h)]]
                + [lambda zz, i=i, d=d: r2y[i, d, zz] for d in range(ny - 1)],
            )
        third.append(
            [send(held.at[to], r3.at[part, slot], at_z(to)) for slot, to in offsets(z, nz)]
        )

    total = n_ref[span(gi, rows)].astype(F32)
    for d in range(1, peers):
        node_copies[d - 1].wait_recv()
        total = total + nodes_in[d - 1].astype(F32)
    node_ref[...] = total

    fourth = []
    for part in parts:
        i = part // 2
        arrive(third[part])
        total = (r2x[i, nx - 1, z] if part % 2 == 0 else r2y[i, ny - 1, z]).astype(F32)
        for d in range(nz - 1):
            total = total + r3[part, d].astype(F32)
        mine = span((part * 2 + core) * ny + y, h)
        out_ref[mine] = (total * (1.0 / ndp)).astype(BF)
        fourth.append(
            [send(out_ref.at[mine], out_ref.at[mine], at_y(to)) for _, to in offsets(y, ny)]
        )
    fifth = []
    for part in parts:
        arrive(fourth[part])
        half = span(part * 2 + core, yh)
        fifth.append(send(out_ref.at[half], out_ref.at[half], other_core))
    arrive(fifth)
    for copy in sent:
        copy.wait_send()


def reduce_all(terms, node_terms, ny, nx, nz):
    peers, rows_padded, ch = terms.shape
    ndp = 2 * ny
    h = rows_padded // (PARTS * ndp)
    rows = node_terms.shape[0] // peers
    sends = 2 * PARTS + (peers - 1) + PARTS * (2 * (ny - 1) + nx - 1 + nz - 1)
    vmem = pl.BlockSpec(memory_space=pltpu.VMEM)
    return pl.pallas_call(
        functools.partial(reduce_kernel, ny, nx, nz, h),
        name="reduce_all",
        out_shape=[
            jax.ShapeDtypeStruct((rows_padded, ch), BF),
            jax.ShapeDtypeStruct((rows, node_terms.shape[1]), F32),
        ],
        in_specs=[pl.BlockSpec(memory_space=pl.ANY), vmem],
        out_specs=[vmem] * 2,
        scratch_shapes=[
            pltpu.VMEM((PARTS, nz, nx, ny * h, ch), BF),
            pltpu.VMEM((PARTS, nz, nx, ny * h, ch), BF),
            pltpu.VMEM((PARTS // 2, ny, nz, nx, h, ch), BF),
            pltpu.VMEM((PARTS // 2, nx, nz, ny * h, ch), BF),
            pltpu.VMEM((PARTS // 2, nx, nz, h, ch), BF),
            pltpu.VMEM((PARTS // 2, ny, nz, h, ch), BF),
            pltpu.VMEM((PARTS, max(nz - 1, 1), h, ch), BF),
            pltpu.VMEM((peers - 1, rows, node_terms.shape[1]), BF),
            pltpu.SemaphoreType.DMA((sends,)),
            pltpu.SemaphoreType.DMA((sends,)),
            pltpu.SemaphoreType.DMA((PARTS,)),
        ],
        compiler_params=pltpu.CompilerParams(
            collective_id=1, has_side_effects=True, vmem_limit_bytes=56 * 2**20
        ),
    )(terms.reshape(nz, nx, rows_padded, ch), node_terms)


def per_device(
    node_features, cotangent, wigner, w_zero, w_one_re, w_one_im, w_two_re, w_two_im, w_attn,
    src_slot, dst_node, request, edge_count,
):
    peers = lax.axis_size("graph")
    ndp = lax.axis_size("dp")
    ny = ndp // 2
    nx = ny
    nz = peers // nx
    nodes, coef, ch = node_features.shape
    heads = w_attn.shape[1]
    plan, used = shard_plan(peers, ch, ch)
    unit = 16 * PARTS * ndp
    rows_padded = -(-used // unit) * unit
    packed = all(rows % 16 == 0 for which, _, _, rows in plan if which < 5)
    packed = packed and plan[-1][3] % 8 == 0

    everyone = gather_nodes(to_rows(node_features), nx, nz)
    results = compute(
        peers, nodes, request.shape[2], heads, plan, rows_padded, packed,
        everyone, to_rows(cotangent), wigner, w_zero, w_one_re, w_one_im, w_two_re, w_two_im,
        jnp.pad(w_attn, ((0, 0), (0, ch - heads))),
        src_slot[None, :], dst_node[None, :], request[0], edge_count,
    )
    node_terms = results[-1]
    if packed:
        terms = results[0]
    else:
        pieces = [
            results[which].reshape(peers, rows, -1)[:, :, cb * ch : (cb + 1) * ch]
            for which, cb, _, rows in plan
        ]
        pieces.append(jnp.zeros((peers, rows_padded - used, ch), BF))
        terms = jnp.concatenate(pieces, axis=1)
    shard, node_rows = reduce_all(terms, node_terms, ny, nx, nz)
    node_grad = from_rows(node_rows, nodes, coef, ch)
    outs = []
    for which in range(5):
        mine = [p for p in plan if p[0] == which]
        at, rows = mine[0][2], mine[0][3]
        block = shard[at : at + rows * len(mine)].reshape(len(mine), rows, ch)
        outs.append(block.transpose(1, 0, 2).reshape(rows, -1).astype(F32))
    _, _, at, rows = plan[-1]
    folded = shard[at : at + rows, : 2 * heads]
    folded = jnp.concatenate([folded[:, :heads], folded[:, heads:]], 0)
    outs.append(folded.astype(F32))
    return (node_grad, *outs)


def solution(mesh):
    both = ("dp", "graph")
    in_specs = (
        P(both, None, None), P(both, None, None), P(None, both),
        P(), P(), P(), P(), P(), P(),
        P(both), P(both), P(both, None, None), P(both),
    )
    out_specs = (P(both, None, None),) + (P("graph", None),) * 6
    return jax.shard_map(
        per_device, mesh=mesh, in_specs=in_specs, out_specs=out_specs, check_vma=False
    )
```

```python
import functools

import jax
import jax.numpy as jnp
from jax import lax
from jax.experimental import pallas as pl
from jax.experimental.pallas import tpu as pltpu
from jax.sharding import PartitionSpec as P

LMAX = 6
MMAX = 2
NCOEF = (LMAX + 1) ** 2
ORDERS = (0, 1, -1, 2, -2)
MESH = pl.DeviceIdType.MESH
BF = jnp.bfloat16
F32 = jnp.float32
QUARTERS = 4
WIDTH = -(-NCOEF // QUARTERS)
CHUNK = 32
PARTS = 4


def block_offset(degree):
    offset = 0
    for lower in range(degree):
        offset += (2 * min(lower, MMAX) + 1) * (2 * lower + 1)
    return offset


def entry_index(degree, order, column):
    row = min(degree, MMAX) + order
    return block_offset(degree) + row * (2 * degree + 1) + column


def dot(left, right, dims, precision=None):
    return lax.dot_general(
        left, right, (dims, ((), ())), preferred_element_type=F32, precision=precision
    )


NN = ((1,), (0,))
NT = ((1,), (1,))
TN = ((0,), (0,))


def to_rows(values):
    nodes, coef, ch = values.shape
    padded = jnp.pad(values, ((0, 0), (0, QUARTERS * WIDTH - coef), (0, 0)))
    return (
        padded.reshape(nodes, QUARTERS, WIDTH * ch)
        .transpose(1, 0, 2)
        .reshape(QUARTERS * nodes, WIDTH * ch)
    )


def from_rows(rows, nodes, coef, ch):
    whole = rows.reshape(QUARTERS, nodes, WIDTH * ch).transpose(1, 0, 2)
    return whole.reshape(nodes, QUARTERS * WIDTH, ch)[:, :coef]


def gather_kernel(nx, nz, x_ref, out_ref, send_sem, recv_sem):
    me = lax.axis_index("graph")
    x, z = lax.rem(me, nx), me // nx
    rows = x_ref.shape[0]
    along_x = [z * nx + lax.rem(x + d, nx) for d in range(1, nx)]
    along_z = [lax.rem(z + d, nz) * nx + x for d in range(1, nz)]
    barrier = pltpu.get_barrier_semaphore()
    for to in along_x + along_z:
        pl.semaphore_signal(barrier, inc=1, device_id={"graph": to}, device_id_type=MESH)
    pl.semaphore_wait(barrier, nx - 1 + nz - 1)

    def block(index):
        return out_ref.at[pl.ds(pl.multiple_of(index * rows, rows), rows)]

    copies = []

    def send(source, index, to):
        i = len(copies)
        copy = pltpu.make_async_remote_copy(
            src_ref=source, dst_ref=block(index), send_sem=send_sem.at[i],
            recv_sem=recv_sem.at[i], device_id={"graph": to}, device_id_type=MESH,
        )
        copy.start()
        copies.append(copy)
        return copy

    over_z = [send(x_ref, me, to) for to in along_z]
    for to in along_x:
        send(x_ref, me, to)
    out_ref[pl.ds(pl.multiple_of(me * rows, rows), rows)] = x_ref[...]
    for d in range(1, nz):
        over_z[d - 1].wait_recv()
        came = lax.rem(z + nz - d, nz) * nx + x
        for to in along_x:
            send(block(came), came, to)
    for i, copy in enumerate(copies):
        copy.wait_send()
        if i >= nz - 1:
            copy.wait_recv()


def gather_nodes(x, nx, nz):
    sends = nz - 1 + (nx - 1) * nz
    return pl.pallas_call(
        functools.partial(gather_kernel, nx, nz),
        name="gather_nodes",
        out_shape=jax.ShapeDtypeStruct((nx * nz * x.shape[0], x.shape[1]), x.dtype),
        in_specs=[pl.BlockSpec(memory_space=pltpu.VMEM)],
        out_specs=pl.BlockSpec(memory_space=pltpu.VMEM),
        scratch_shapes=[
            pltpu.SemaphoreType.DMA((sends,)),
            pltpu.SemaphoreType.DMA((sends,)),
        ],
        compiler_params=pltpu.CompilerParams(
            collective_id=0, has_side_effects=True, vmem_limit_bytes=24 * 2**20
        ),
    )(x)


def shard_plan(peers, ch, heads_padded):
    plan, at = [], 0
    for which, degrees in enumerate((LMAX + 1, LMAX, LMAX, LMAX - 1, LMAX - 1)):
        rows = degrees * ch // peers
        for cb in range(degrees):
            plan.append((which, cb, at, rows))
            at += rows
    rows = (LMAX + 1) * ch // peers // 2
    plan.append((5, 0, at, rows))
    return plan, at + rows


def compute_kernel(
    peers, nodes, slots, heads, plan, packed,
    g_ref, cot_ref, wig_ref, wz_ref, w1r_ref, w1i_ref, w2r_ref, w2i_ref, wa_ref,
    src_ref, dst_ref, req_ref, count_ref,
    *rest,
):
    if packed:
        (t_ref, n_ref), rest = rest[:2], rest[2:]
    else:
        (tz_ref, t1r_ref, t1i_ref, t2r_ref, t2i_ref, ta_ref, n_ref), rest = rest[:7], rest[7:]
    (srcT, cotT, izT, i1T, i2T, iz, i1, i2, bT, oh_s, igT, sgT, gz, g1, g2, bk) = rest
    ch = 128
    edges = src_ref.shape[1]
    per = QUARTERS * nodes
    k = peers * per

    src = src_ref[...]
    base = jnp.zeros((1, edges), jnp.int32)
    for s in range(peers * slots):
        base = jnp.where(src == s, (s // slots) * per + req_ref[s // slots, s % slots], base)
    iota_k = lax.broadcasted_iota(jnp.int32, (k, edges), 0)
    for q in range(QUARTERS):
        hot = jnp.where(iota_k == base + q * nodes, 1.0, 0.0).astype(BF)
        oh_s[q] = hot
        srcT[pl.ds(q * WIDTH * ch, WIDTH * ch), :] = dot(g_ref[...], hot, TN)
    live = lax.broadcasted_iota(jnp.int32, (1, edges), 1) < count_ref[0]
    target = jnp.where(live, dst_ref[...], -per)
    iota_c = lax.broadcasted_iota(jnp.int32, (per, edges), 0)
    for q in range(QUARTERS):
        hot = jnp.where(iota_c == target + q * nodes, 1.0, 0.0).astype(BF)
        cotT[pl.ds(q * WIDTH * ch, WIDTH * ch), :] = dot(cot_ref[...], hot, TN)

    firsts = {0: 0, 1: LMAX + 1, -1: 2 * LMAX + 1, 2: 3 * LMAX + 1, -2: 4 * LMAX}

    def block_of(degree, order):
        return firsts[order] + degree - abs(order)

    def rotate_step(step, carry):
        at = step * CHUNK
        for degree in range(LMAX + 1):
            reach = min(degree, MMAX)
            for source, is_cot in ((srcT, False), (cotT, True)):
                acc = {}
                for column in range(2 * degree + 1):
                    row0 = (degree * degree + column) * ch
                    value = source[pl.ds(pl.multiple_of(row0 + at, CHUNK), CHUNK), :]
                    for order in range(-reach, reach + 1):
                        index = entry_index(degree, order, column)
                        term = wig_ref[index : index + 1, :] * value
                        acc[order] = acc[order] + term if order in acc else term
                for order in range(-reach, reach + 1):
                    if is_cot:
                        row0 = block_of(degree, order) * ch
                        bT[pl.ds(pl.multiple_of(row0 + at, CHUNK), CHUNK), :] = acc[order]
                        continue
                    row0 = (degree - abs(order)) * ch
                    rows = pl.ds(pl.multiple_of(row0 + at, CHUNK), CHUNK)
                    rounded = acc[order].astype(BF)
                    if order == 0:
                        izT[rows, :] = rounded
                    else:
                        half = 0 if order > 0 else edges
                        held = i1T if abs(order) == 1 else i2T
                        held[rows, half : half + edges] = rounded
        return carry

    lax.fori_loop(0, ch // CHUNK, rotate_step, 0)

    def turn(block):
        return jnp.transpose(block)

    for j in range(LMAX + 1):
        cols = slice(j * ch, (j + 1) * ch)
        iz[:, cols] = turn(izT[cols, :].astype(F32)).astype(BF)
    for j in range(LMAX):
        cols = slice(j * ch, (j + 1) * ch)
        for half in range(2):
            lanes = slice(half * edges, (half + 1) * edges)
            i1[lanes, cols] = turn(i1T[cols, lanes].astype(F32)).astype(BF)
            if j < LMAX - 1:
                i2[lanes, cols] = turn(i2T[cols, lanes].astype(F32)).astype(BF)
    blocks = 5 * LMAX - 1
    for j in range(blocks):
        bk[j] = turn(bT[j * ch : (j + 1) * ch, :])

    out_zero = dot(iz[...], wz_ref[...], NN)
    zero_rounded = out_zero.astype(BF)
    agreement = jnp.zeros((edges, ch), F32)
    for j in range(LMAX + 1):
        agreement = agreement + bk[j] * out_zero[:, j * ch : (j + 1) * ch]
    for order, degrees, held, re_ref, im_ref in (
        (1, LMAX, i1, w1r_ref, w1i_ref),
        (2, LMAX - 1, i2, w2r_ref, w2i_ref),
    ):
        with_re = dot(held[...], re_ref[...], NN)
        with_im = dot(held[...], im_ref[...], NN)
        out_p = with_re[:edges] - with_im[edges:]
        out_n = with_im[:edges] + with_re[edges:]
        for j in range(degrees):
            cols = slice(j * ch, (j + 1) * ch)
            agreement = agreement + bk[firsts[order] + j] * out_p[:, cols]
            agreement = agreement + bk[firsts[-order] + j] * out_n[:, cols]

    wa = wa_ref[...]
    weighting = jax.nn.sigmoid(dot(zero_rounded, wa, NN))
    head_of = lax.broadcasted_iota(jnp.int32, (ch, ch), 0) // (ch // heads)
    member = jnp.where(head_of == lax.broadcasted_iota(jnp.int32, (ch, ch), 1), 1.0, 0.0)
    exact = lax.Precision.HIGHEST
    head_sum = dot(agreement, member, NN, exact)
    logit_grad = (head_sum * weighting * (1.0 - weighting)).astype(BF)
    spread = dot(weighting, member, NT, exact)

    from_logit = dot(logit_grad, wa, NT)
    for j in range(LMAX + 1):
        cols = slice(j * ch, (j + 1) * ch)
        gz[:, cols] = (bk[j] * spread + from_logit[:, cols]).astype(BF)
    for order, degrees, held in ((1, LMAX, g1), (2, LMAX - 1, g2)):
        for j in range(degrees):
            cols = slice(j * ch, (j + 1) * ch)
            plus = (bk[firsts[order] + j] * spread).astype(BF)
            minus = (bk[firsts[-order] + j] * spread).astype(BF)
            held[0:edges, cols] = plus
            held[edges : 2 * edges, cols] = minus
            held[2 * edges : 3 * edges, cols] = -plus

    terms = (
        (0, lambda: dot(izT[...], gz[...], NN)),
        (1, lambda: dot(i1T[...], g1[0 : 2 * edges, :], NN)),
        (2, lambda: dot(i1T[...], g1[edges : 3 * edges, :], NN)),
        (3, lambda: dot(i2T[...], g2[0 : 2 * edges, :], NN)),
        (4, lambda: dot(i2T[...], g2[edges : 3 * edges, :], NN)),
        (5, lambda: dot(zero_rounded, logit_grad, TN)),
    )
    for which, make in terms:
        value = make()
        if which == 5:
            value = value.reshape(peers, 2, -1, ch)
            value = value[:, 0] + pltpu.roll(value[:, 1].reshape(-1, ch), heads, 1).reshape(
                peers, -1, ch
            )
            if packed:
                at, rows = plan[-1][2:]
                spare = t_ref.shape[1] - at - rows
                if spare:
                    value = jnp.concatenate([value, jnp.zeros((peers, spare, ch), F32)], 1)
                t_ref[:, at:, :] = value.astype(BF)
                continue
            value = value.reshape(-1, ch)
        value = value.astype(BF)
        if not packed:
            (tz_ref, t1r_ref, t1i_ref, t2r_ref, t2i_ref, ta_ref)[which][...] = value
            continue
        for owner, cb, at, rows in plan:
            if owner != which:
                continue
            for g in range(peers):
                t_ref[g, at : at + rows, :] = value[
                    g * rows : (g + 1) * rows, cb * ch : (cb + 1) * ch
                ]
    def put(block, degrees, value):
        igT[block * ch : (block + degrees) * ch, :] = value

    put(0, LMAX + 1, dot(wz_ref[...], gz[...], NT))
    for order, degrees, held, re_ref, im_ref in (
        (1, LMAX, g1, w1r_ref, w1i_ref),
        (2, LMAX - 1, g2, w2r_ref, w2i_ref),
    ):
        both = held[0 : 2 * edges, :]
        with_re = dot(re_ref[...], both, NT)
        with_im = dot(im_ref[...], both, NT)
        put(firsts[order], degrees, with_re[:, :edges] + with_im[:, edges:])
        put(firsts[-order], degrees, with_re[:, edges:] - with_im[:, :edges])

    def unrotate_step(step, carry):
        at = step * CHUNK
        for degree in range(LMAX + 1):
            reach = min(degree, MMAX)
            held = {}
            for order in range(-reach, reach + 1):
                row0 = block_of(degree, order) * ch
                held[order] = igT[pl.ds(pl.multiple_of(row0 + at, CHUNK), CHUNK), :]
            for column in range(2 * degree + 1):
                total = None
                for order in range(-reach, reach + 1):
                    index = entry_index(degree, order, column)
                    term = wig_ref[index : index + 1, :] * held[order]
                    total = term if total is None else total + term
                row0 = (degree * degree + column) * ch
                sgT[pl.ds(pl.multiple_of(row0 + at, CHUNK), CHUNK), :] = total.astype(BF)
        return carry

    lax.fori_loop(0, ch // CHUNK, unrotate_step, 0)
    tail = QUARTERS * WIDTH - NCOEF
    if tail:
        sgT[NCOEF * ch : (NCOEF + tail) * ch, :] = jnp.zeros((tail * ch, edges), BF)
    total = None
    for q in range(QUARTERS):
        part = dot(oh_s[q], sgT[q * WIDTH * ch : (q + 1) * WIDTH * ch, :], NT)
        total = part if total is None else total + part
    n_ref[...] = total.astype(BF)


def compute(peers, nodes, slots, heads, plan, rows_padded, packed, *args):
    ch = 128
    edges = args[9].shape[1]
    wide, mid, low = (LMAX + 1) * ch, LMAX * ch, (LMAX - 1) * ch
    blocks = 5 * LMAX - 1
    k = peers * QUARTERS * nodes
    if packed:
        outs = [jax.ShapeDtypeStruct((peers, rows_padded, ch), BF)]
    else:
        outs = [
            jax.ShapeDtypeStruct(shape, BF)
            for shape in ((wide, wide), (mid, mid), (mid, mid), (low, low), (low, low), (wide // 2, ch))
        ]
    outs.append(jax.ShapeDtypeStruct((k, WIDTH * ch), BF))
    vmem = pl.BlockSpec(memory_space=pltpu.VMEM)
    smem = pl.BlockSpec(memory_space=pltpu.SMEM)
    coefs = QUARTERS * WIDTH * ch
    return pl.pallas_call(
        functools.partial(compute_kernel, peers, nodes, slots, heads, plan, packed),
        name="edge_backward",
        out_shape=outs,
        in_specs=[vmem] * 11 + [smem] * 2,
        out_specs=[vmem] * len(outs),
        scratch_shapes=[
            pltpu.VMEM((coefs, edges), F32),
            pltpu.VMEM((coefs, edges), F32),
            pltpu.VMEM((wide, edges), BF),
            pltpu.VMEM((mid, 2 * edges), BF),
            pltpu.VMEM((low, 2 * edges), BF),
            pltpu.VMEM((edges, wide), BF),
            pltpu.VMEM((2 * edges, mid), BF),
            pltpu.VMEM((2 * edges, low), BF),
            pltpu.VMEM((blocks * ch, edges), F32),
            pltpu.VMEM((QUARTERS, k, edges), BF),
            pltpu.VMEM((blocks * ch, edges), F32),
            pltpu.VMEM((coefs, edges), BF),
            pltpu.VMEM((edges, wide), BF),
            pltpu.VMEM((3 * edges, mid), BF),
            pltpu.VMEM((3 * edges, low), BF),
            pltpu.VMEM((blocks, edges, ch), F32),
        ],
        compiler_params=pltpu.CompilerParams(vmem_limit_bytes=48 * 2**20),
    )(*args)


def reduce_kernel(
    ny, nx, nz, h,
    t_ref, n_ref, out_ref, node_ref,
    own, r0, r1y, r1x, r2x, r2y, r3, nodes_in, send_sem, recv_sem, own_sem,
):
    dp = lax.axis_index("dp")
    gi = lax.axis_index("graph")
    core, y = lax.rem(dp, 2), dp // 2
    x, z = lax.rem(gi, nx), gi // nx
    peers = nx * nz
    ndp = 2 * ny
    yh = ny * h

    def at_y(v):
        return {"dp": v * 2 + core}

    def at_x(v):
        return {"graph": z * nx + v}

    def at_z(v):
        return {"graph": v * nx + x}

    other_core = {"dp": y * 2 + 1 - core}

    def span(index, size):
        return pl.ds(pl.multiple_of(index * size, 16), size)

    locals_ = []
    for part in range(PARTS):
        copy = pltpu.make_async_copy(
            t_ref.at[:, :, span(part * 2 + core, yh)], own.at[part], own_sem.at[part]
        )
        copy.start()
        locals_.append(copy)

    barrier = pltpu.get_barrier_semaphore()
    for d in range(1, ndp):
        pl.semaphore_signal(
            barrier, inc=1, device_id={"dp": lax.rem(dp + d, ndp)}, device_id_type=MESH
        )
    for d in range(1, peers):
        pl.semaphore_signal(
            barrier, inc=1, device_id={"graph": lax.rem(gi + d, peers)}, device_id_type=MESH
        )
    pl.semaphore_wait(barrier, ndp - 1 + peers - 1)

    sent = []

    def send(source, target, device):
        i = len(sent)
        copy = pltpu.make_async_remote_copy(
            src_ref=source, dst_ref=target, send_sem=send_sem.at[i], recv_sem=recv_sem.at[i],
            device_id=device, device_id_type=MESH,
        )
        copy.start()
        sent.append(copy)
        return copy

    def arrive(copies):
        for copy in copies:
            copy.wait_recv()

    def offsets(me, n):
        return [(d - 1, lax.rem(me + d, n)) for d in range(1, n)]

    def sum_over_z(target, sources):
        def step(zz, carry):
            total = None
            for source in sources:
                value = source(zz).astype(F32)
                total = value if total is None else total + value
            target[zz] = total.astype(BF)
            return carry

        lax.fori_loop(0, nz, step, 0)

    parts = range(PARTS)
    zero = [
        send(t_ref.at[:, :, span(part * 2 + (1 - core), yh)], r0.at[part], other_core)
        for part in parts
    ]
    rows = node_ref.shape[0]
    node_copies = []
    for slot, to in offsets(gi, peers):
        node_copies.append(send(n_ref.at[span(to, rows)], nodes_in.at[slot], {"graph": to}))

    first = []
    for part in parts:
        i = part // 2
        locals_[part].wait()
        zero[part].wait_recv()
        sum_over_z(
            r0.at[part],
            [lambda zz, part=part: own[part, zz], lambda zz, part=part: r0[part, zz]],
        )
        if part % 2 == 0:
            first.append(
                [send(r0.at[part, :, :, span(to, h)], r1y.at[i, slot], at_y(to))
                 for slot, to in offsets(y, ny)]
            )
        else:
            first.append(
                [send(r0.at[part, :, to], r1x.at[i, slot], at_x(to))
                 for slot, to in offsets(x, nx)]
            )

    second = []
    for part in parts:
        i = part // 2
        arrive(first[part])
        if part % 2 == 0:
            sum_over_z(
                r1y.at[i, ny - 1],
                [lambda zz, part=part: r0[part, zz, :, span(y, h)]]
                + [lambda zz, i=i, d=d: r1y[i, d, zz] for d in range(ny - 1)],
            )
            second.append(
                [send(r1y.at[i, ny - 1, :, to], r2x.at[i, slot], at_x(to))
                 for slot, to in offsets(x, nx)]
            )
        else:
            sum_over_z(
                r1x.at[i, nx - 1],
                [lambda zz, part=part: r0[part, zz, x]]
                + [lambda zz, i=i, d=d: r1x[i, d, zz] for d in range(nx - 1)],
            )
            second.append(
                [send(r1x.at[i, nx - 1, :, span(to, h)], r2y.at[i, slot], at_y(to))
                 for slot, to in offsets(y, ny)]
            )

    third = []
    for part in parts:
        i = part // 2
        arrive(second[part])
        if part % 2 == 0:
            held = r2x.at[i, nx - 1]
            sum_over_z(
                held,
                [lambda zz, i=i: r1y[i, ny - 1, zz, x]]
                + [lambda zz, i=i, d=d: r2x[i, d, zz] for d in range(nx - 1)],
            )
        else:
            held = r2y.at[i, ny - 1]
            sum_over_z(
                held,
                [lambda zz, i=i: r1x[i, nx - 1, zz, span(y, h)]]
                + [lambda zz, i=i, d=d: r2y[i, d, zz] for d in range(ny - 1)],
            )
        third.append(
            [send(held.at[to], r3.at[part, slot], at_z(to)) for slot, to in offsets(z, nz)]
        )

    total = n_ref[span(gi, rows)].astype(F32)
    for d in range(1, peers):
        node_copies[d - 1].wait_recv()
        total = total + nodes_in[d - 1].astype(F32)
    node_ref[...] = total

    fourth = []
    for part in parts:
        i = part // 2
        arrive(third[part])
        total = (r2x[i, nx - 1, z] if part % 2 == 0 else r2y[i, ny - 1, z]).astype(F32)
        for d in range(nz - 1):
            total = total + r3[part, d].astype(F32)
        mine = span((part * 2 + core) * ny + y, h)
        out_ref[mine] = (total * (1.0 / ndp)).astype(BF)
        fourth.append(
            [send(out_ref.at[mine], out_ref.at[mine], at_y(to)) for _, to in offsets(y, ny)]
        )
    fifth = []
    for part in parts:
        arrive(fourth[part])
        half = span(part * 2 + core, yh)
        fifth.append(send(out_ref.at[half], out_ref.at[half], other_core))
    arrive(fifth)
    for copy in sent:
        copy.wait_send()


def reduce_all(terms, node_terms, ny, nx, nz):
    peers, rows_padded, ch = terms.shape
    ndp = 2 * ny
    h = rows_padded // (PARTS * ndp)
    rows = node_terms.shape[0] // peers
    sends = 2 * PARTS + (peers - 1) + PARTS * (2 * (ny - 1) + nx - 1 + nz - 1)
    vmem = pl.BlockSpec(memory_space=pltpu.VMEM)
    return pl.pallas_call(
        functools.partial(reduce_kernel, ny, nx, nz, h),
        name="reduce_all",
        out_shape=[
            jax.ShapeDtypeStruct((rows_padded, ch), BF),
            jax.ShapeDtypeStruct((rows, node_terms.shape[1]), F32),
        ],
        in_specs=[pl.BlockSpec(memory_space=pl.ANY), vmem],
        out_specs=[vmem] * 2,
        scratch_shapes=[
            pltpu.VMEM((PARTS, nz, nx, ny * h, ch), BF),
            pltpu.VMEM((PARTS, nz, nx, ny * h, ch), BF),
            pltpu.VMEM((PARTS // 2, ny, nz, nx, h, ch), BF),
            pltpu.VMEM((PARTS // 2, nx, nz, ny * h, ch), BF),
            pltpu.VMEM((PARTS // 2, nx, nz, h, ch), BF),
            pltpu.VMEM((PARTS // 2, ny, nz, h, ch), BF),
            pltpu.VMEM((PARTS, max(nz - 1, 1), h, ch), BF),
            pltpu.VMEM((peers - 1, rows, node_terms.shape[1]), BF),
            pltpu.SemaphoreType.DMA((sends,)),
            pltpu.SemaphoreType.DMA((sends,)),
            pltpu.SemaphoreType.DMA((PARTS,)),
        ],
        compiler_params=pltpu.CompilerParams(
            collective_id=1, has_side_effects=True, vmem_limit_bytes=51 * 2**20
        ),
    )(terms.reshape(nz, nx, rows_padded, ch), node_terms)


def per_device(
    node_features, cotangent, wigner, w_zero, w_one_re, w_one_im, w_two_re, w_two_im, w_attn,
    src_slot, dst_node, request, edge_count,
):
    peers = lax.axis_size("graph")
    ndp = lax.axis_size("dp")
    ny = ndp // 2
    nx = ny
    nz = peers // nx
    nodes, coef, ch = node_features.shape
    heads = w_attn.shape[1]
    plan, used = shard_plan(peers, ch, ch)
    unit = 16 * PARTS * ndp
    rows_padded = -(-used // unit) * unit
    packed = all(rows % 16 == 0 for which, _, _, rows in plan if which < 5)
    packed = packed and plan[-1][3] % 8 == 0

    everyone = gather_nodes(to_rows(node_features), nx, nz)
    results = compute(
        peers, nodes, request.shape[2], heads, plan, rows_padded, packed,
        everyone, to_rows(cotangent), wigner, w_zero, w_one_re, w_one_im, w_two_re, w_two_im,
        jnp.pad(w_attn, ((0, 0), (0, ch - heads))),
        src_slot[None, :], dst_node[None, :], request[0], edge_count,
    )
    node_terms = results[-1]
    if packed:
        terms = results[0]
    else:
        pieces = [
            results[which].reshape(peers, rows, -1)[:, :, cb * ch : (cb + 1) * ch]
            for which, cb, _, rows in plan
        ]
        pieces.append(jnp.zeros((peers, rows_padded - used, ch), BF))
        terms = jnp.concatenate(pieces, axis=1)
    shard, node_rows = reduce_all(terms, node_terms, ny, nx, nz)
    node_grad = from_rows(node_rows, nodes, coef, ch)
    outs = []
    for which in range(5):
        mine = [p for p in plan if p[0] == which]
        at, rows = mine[0][2], mine[0][3]
        block = shard[at : at + rows * len(mine)].reshape(len(mine), rows, ch)
        outs.append(block.transpose(1, 0, 2).reshape(rows, -1).astype(F32))
    _, _, at, rows = plan[-1]
    folded = shard[at : at + rows, : 2 * heads]
    folded = jnp.concatenate([folded[:, :heads], folded[:, heads:]], 0)
    outs.append(folded.astype(F32))
    return (node_grad, *outs)


def solution(mesh):
    both = ("dp", "graph")
    in_specs = (
        P(both, None, None), P(both, None, None), P(None, both),
        P(), P(), P(), P(), P(), P(),
        P(both), P(both), P(both, None, None), P(both),
    )
    out_specs = (P(both, None, None),) + (P("graph", None),) * 6
    return jax.shard_map(
        per_device, mesh=mesh, in_specs=in_specs, out_specs=out_specs, check_vma=False
    )
```
